32 devices in a mesh: grp: 2 (over y), row: 16 (over z, x, core), kc: 1.
Axes of the slice: x: 2, y: 2, z: 4, core: 2. Of those that a mesh axis runs over, the one named last changes fastest.
Arguments:
- pair: bfloat16 [256, 128, 128], P(('grp', 'row'), 'kc'), parts along dimension 0, may hold values from -6 to 6
- w_in: bfloat16 [2, 128, 512], replicated, may hold values from -0.5 to 0.5
- w_gate: bfloat16 [2, 128, 128], replicated, may hold values from -0.5 to 0.5
- w_out: bfloat16 [2, 128, 128], replicated, may hold values from -0.5 to 0.5
- gain_in: float32 [2, 128], replicated, may hold values from 0.25 to 1.75
- bias_in: float32 [2, 128], replicated, may hold values from -0.6 to 0.6
- gain_mid: float32 [2, 128], replicated, may hold values from 0.25 to 1.75
- bias_mid: float32 [2, 128], replicated, may hold values from -0.6 to 0.6
Outputs:
- updated: bfloat16 [256, 128, 128], P(('grp', 'row'), 'kc'), parts along dimension 0
- incoming_mid: bfloat16 [256, 128, 128], P(('grp', 'row'), 'kc'), parts along dimension 0
The draws below stay inside these ranges and needn't reach their ends.
There are 2 independent parts, one for each index of `grp`. The reference program is written for one: setup_inputs(seed, part) draws one part's arguments, and reference() takes and returns one part's arrays. A program takes and returns all parts, laid end to end along the dimension named above; an argument that names none is the same for every part. Nothing has to cross between parts.
All inputs are finite; a program needn't handle non-finite values.
Results may differ from the reference program's by a relative error of at most 0.025.
Values may be sent and summed in bfloat16 or wider, within the bound.
A program may use at most 64 MiB of HBM per device.

```python
import math
import jax
import jax.numpy as jnp
from jax import lax

C = 128
HID = 128
N = 128


def block_levels(rng, extent, shards, low, largest):
    factor_of, own = 1.0, jax.random.fold_in(rng, 6)
    for position, shards_of in shards:
        heights = jnp.exp(jax.random.uniform(jax.random.fold_in(own, position), (shards_of,), jnp.float32, low / len(shards), largest / len(shards)))
        factor_of = factor_of * jnp.repeat(heights, extent[position] // shards_of).reshape([-1 if axis == position else 1 for axis in range(len(extent))])
    return factor_of


def noise(stream_key, shape, deviation, bound, cuts=(), kind=jnp.bfloat16):
    drawn = jax.random.normal(stream_key, shape, jnp.float32) * deviation
    if len(cuts) > 0:
        drawn = block_levels(stream_key, shape, cuts, -0.22, 0.18) * drawn
    return jnp.clip(drawn, min=-bound, max=bound).astype(kind)


def setup_inputs(seed: int = 0, part: int = 0) -> dict:
    splits = jax.random.split(jax.random.key(seed), 9)
    own_keys = jax.random.split(jax.random.fold_in(splits[8], part), 9)
    pair = noise(own_keys[0], (N, N, C), 1.0, 6.0, ((0, 16),))
    w_in = noise(splits[1], (2, C, 4 * HID), C ** -0.5, 0.5)
    w_gate = noise(splits[2], (2, C, C), C ** -0.5, 0.5)
    w_out = noise(splits[3], (2, HID, C), HID ** -0.5, 0.5)
    gain_in = jnp.clip(1.0 + 0.15 * jax.random.normal(splits[4], (2, C), jnp.float32), 0.25, 1.75)
    bias_in = noise(splits[5], (2, C), 0.1, 0.6, (), jnp.float32)
    gain_mid = jnp.clip(1.0 + 0.15 * jax.random.normal(splits[6], (2, HID), jnp.float32), 0.25, 1.75)
    bias_mid = noise(splits[7], (2, HID), 0.1, 0.6, (), jnp.float32)
    return dict(pair=pair, w_in=w_in, w_gate=w_gate, w_out=w_out, gain_in=gain_in, bias_in=bias_in, gain_mid=gain_mid, bias_mid=bias_mid)


def layer_norm(values, gain, bias):
    center = lax.optimization_barrier(jnp.mean(values, axis=-1, keepdims=True))
    spread = lax.optimization_barrier(jnp.mean((values - center) ** 2, axis=-1, keepdims=True))
    return (values - center) * lax.rsqrt(spread + 1e-05) * gain + bias

def triangle(state, layer_index, w_in, w_gate, w_out, gain_in, bias_in, gain_mid, bias_mid, incoming):
    block = math.gcd(N, 64)
    blocks = N // block
    weights_in = w_in[layer_index]
    weights_gate = w_gate[layer_index]
    weights_out = w_out[layer_index]

    def project(pair_rows):
        normed = layer_norm(pair_rows.astype(jnp.float32), gain_in[layer_index], bias_in[layer_index]).astype(jnp.bfloat16)
        projected = jnp.dot(normed.reshape(-1, C), weights_in, preferred_element_type=jnp.float32)
        left = (jax.nn.sigmoid(projected[:, :HID]) * projected[:, HID:2 * HID]).astype(jnp.bfloat16)
        right = (jax.nn.sigmoid(projected[:, 2 * HID:3 * HID]) * projected[:, 3 * HID:]).astype(jnp.bfloat16)
        return (left.reshape(block, N, HID), right.reshape(block, N, HID))
    left, right = lax.map(project, state.reshape(blocks, block, N, C))
    left = left.reshape(N, N, HID).transpose(2, 0, 1)
    right = right.reshape(N, N, HID).transpose(2, 0, 1)

    def channel(pieces):
        left_c, right_c = pieces
        if incoming:
            return jnp.dot(left_c.T, right_c, preferred_element_type=jnp.float32).astype(jnp.bfloat16)
        return jnp.dot(left_c, right_c.T, preferred_element_type=jnp.float32).astype(jnp.bfloat16)
    summed = lax.map(channel, (left, right))
    summed = summed.transpose(1, 2, 0).reshape(blocks, block, N, HID)

    def finish(pieces):
        pair_rows, tri_rows = pieces
        pair_float = pair_rows.astype(jnp.float32).reshape(-1, C)
        normed = layer_norm(pair_float, gain_in[layer_index], bias_in[layer_index]).astype(jnp.bfloat16)
        gate_values = jax.nn.sigmoid(jnp.dot(normed, weights_gate, preferred_element_type=jnp.float32))
        middle = layer_norm(tri_rows.astype(jnp.float32).reshape(-1, HID), gain_mid[layer_index], bias_mid[layer_index]).astype(jnp.bfloat16)
        branch = jnp.dot(middle, weights_out, preferred_element_type=jnp.float32)
        new_rows = (pair_float + gate_values * branch).astype(jnp.bfloat16).reshape(block, N, C)
        return (new_rows, middle.reshape(block, N, HID))
    new_state, middle = lax.map(finish, (state.reshape(blocks, block, N, C), summed))
    return (new_state.reshape(N, N, C), middle.reshape(N, N, HID))

def reference(pair, w_in, w_gate, w_out, gain_in, bias_in, gain_mid, bias_mid):
    state, unused = triangle(pair, 0, w_in, w_gate, w_out, gain_in, bias_in, gain_mid, bias_mid, False)
    state, middle = triangle(state, 1, w_in, w_gate, w_out, gain_in, bias_in, gain_mid, bias_mid, True)
    return (state, middle)
```

```python
import functools

import jax
import jax.numpy as jnp
from jax import lax
from jax.experimental import pallas as pl
from jax.experimental.pallas import tpu as pltpu
from jax.sharding import PartitionSpec as P


def layer_norm(values, gain, bias, axis_pos):
    center = jnp.mean(values, axis=axis_pos, keepdims=True)
    spread = jnp.mean((values - center) ** 2, axis=axis_pos, keepdims=True)
    return (values - center) * lax.rsqrt(spread + 1e-05) * gain + bias


def prepare(state, layer_index, w_in, w_gate, gain_in, bias_in):
    hidden = w_in.shape[2] // 4
    pair_float = state.astype(jnp.float32)
    normed = layer_norm(pair_float, gain_in[layer_index], bias_in[layer_index], 2).astype(
        jnp.bfloat16
    )
    projected = jnp.einsum(
        "ijc,ch->hij", normed, w_in[layer_index], preferred_element_type=jnp.float32
    )
    left = (jax.nn.sigmoid(projected[:hidden]) * projected[hidden : 2 * hidden]).astype(
        jnp.bfloat16
    )
    right = (jax.nn.sigmoid(projected[2 * hidden : 3 * hidden]) * projected[3 * hidden :]).astype(
        jnp.bfloat16
    )
    gate_values = jax.nn.sigmoid(
        jnp.einsum("ijc,cd->ijd", normed, w_gate[layer_index], preferred_element_type=jnp.float32)
    )
    return (pair_float, left, right, gate_values)


def finish(pair_float, gate_values, returned, layer_index, w_out, gain_mid, bias_mid):
    middle = layer_norm(
        returned.astype(jnp.float32),
        gain_mid[layer_index][:, None],
        bias_mid[layer_index][:, None],
        1,
    ).astype(jnp.bfloat16)
    branch = jnp.einsum(
        "jhi,hc->ijc", middle, w_out[layer_index], preferred_element_type=jnp.float32
    )
    return ((pair_float + gate_values * branch).astype(jnp.bfloat16), middle)


def shards(pair, w_in, w_gate, w_out, gain_in, bias_in, gain_mid, bias_mid):
    pair_float, left, right, gate_values = prepare(pair, 0, w_in, w_gate, gain_in, bias_in)
    left_c, right_c = (
        lax.all_to_all(left, "row", split_axis=0, concat_axis=1, tiled=True),
        lax.all_to_all(right, "row", split_axis=0, concat_axis=1, tiled=True),
    )
    right_rows = right_c
    summed = lax.psum_scatter(
        jnp.einsum("hjs,his->jhi", right_rows, left_c, preferred_element_type=jnp.float32).astype(
            jnp.bfloat16
        ),
        "kc",
        scatter_dimension=0,
        tiled=True,
    ).astype(jnp.float32)
    returned = lax.all_to_all(
        summed.astype(jnp.bfloat16), "row", split_axis=2, concat_axis=1, tiled=True
    )
    state, unused = finish(pair_float, gate_values, returned, 0, w_out, gain_mid, bias_mid)
    pair_float, left, right, gate_values = prepare(state, 1, w_in, w_gate, gain_in, bias_in)
    left_c, right_c = (
        lax.all_to_all(left, "row", split_axis=0, concat_axis=1, tiled=True),
        lax.all_to_all(right, "row", split_axis=0, concat_axis=1, tiled=True),
    )
    summed = jnp.einsum(
        "hpj,hpi->jhi",
        right_c,
        lax.all_gather(left_c, "kc", axis=2, tiled=True),
        preferred_element_type=jnp.float32,
    )
    returned = lax.all_to_all(
        summed.astype(jnp.bfloat16), "row", split_axis=2, concat_axis=1, tiled=True
    )
    final_state, middle = finish(pair_float, gate_values, returned, 1, w_out, gain_mid, bias_mid)
    return (final_state, middle.transpose(2, 0, 1))

MESH = pl.DeviceIdType.MESH
F32 = jnp.float32
BF16 = jnp.bfloat16


def sigmoid(x):
    return 0.5 * jnp.tanh(0.5 * x) + 0.5


def norm_lanes(x, gain, bias):
    center = jnp.mean(x, axis=-1, keepdims=True)
    moved = x - center
    spread = jnp.mean(moved * moved, axis=-1, keepdims=True)
    return moved * lax.rsqrt(spread + 1e-05) * gain + bias


def fused_kernel(
    n,
    pair_ref,
    w_in_ref,
    w_gate_ref,
    w_out_ref,
    gain_in_ref,
    bias_in_ref,
    gain_mid_ref,
    bias_mid_ref,
    out_ref,
    mid_ref,
    w_t,
    state,
    normed,
    gate,
    lanes_l,
    lanes_r,
    send_a,
    recv_a,
    send_b,
    recv_b,
    sa_sem,
    ra_sem,
    sb_sem,
    rb_sem,
):
    rows, tokens, channels = pair_ref.shape
    hidden = w_out_ref.shape[1]
    hb = hidden // n
    part = hb * rows
    me = lax.axis_index("row")

    barrier = pltpu.get_barrier_semaphore()

    def greet(o, c):
        pl.semaphore_signal(
            barrier, inc=1, device_id={"row": lax.rem(me + o, n)}, device_id_type=MESH
        )
        return c

    lax.fori_loop(1, n, greet, 0)

    def copy_to(send, recv, ssem, rsem, u, other):
        return pltpu.make_async_remote_copy(
            src_ref=send.at[u, other],
            dst_ref=recv.at[u, me],
            send_sem=ssem.at[u, other],
            recv_sem=rsem.at[u, me],
            device_id={"row": other},
            device_id_type=MESH,
        )

    def copy_from(send, recv, ssem, rsem, u, other):
        return pltpu.make_async_remote_copy(
            src_ref=send.at[u, other],
            dst_ref=recv.at[u, other],
            send_sem=ssem.at[u, other],
            recv_sem=rsem.at[u, other],
            device_id={"row": other},
            device_id_type=MESH,
        )

    def start_all(bufs, u):
        def body(o, c):
            copy_to(*bufs, u, lax.rem(me + o, n)).start()
            return c

        lax.fori_loop(1, n, body, 0)

    def wait_all(bufs, u):
        def body(o, c):
            copy_from(*bufs, u, lax.rem(me + n - o, n)).wait_recv()
            return c

        lax.fori_loop(1, n, body, 0)

    def drain(bufs, u):
        def body(o, c):
            copy_to(*bufs, u, lax.rem(me + o, n)).wait_send()
            return c

        lax.fori_loop(1, n, body, 0)

    bufs_a = (send_a, recv_a, sa_sem, ra_sem)
    bufs_b = (send_b, recv_b, sb_sem, rb_sem)

    for u in range(2):
        w_t[u] = w_in_ref[u].T

    for u in range(2):
        source = pair_ref if u == 0 else state
        for i in range(rows):
            x = source[i].astype(F32)
            nrm = norm_lanes(x, gain_in_ref[u : u + 1, :], bias_in_ref[u : u + 1, :]).astype(BF16)
            normed[i] = nrm
            proj = lax.dot_general(
                w_t[u], nrm, (((1,), (1,)), ((), ())), preferred_element_type=F32
            )
            lanes_l[pl.ds(i, hidden, stride=rows), :] = (
                sigmoid(proj[:hidden]) * proj[hidden : 2 * hidden]
            )
            lanes_r[pl.ds(i, hidden, stride=rows), :] = (
                sigmoid(proj[2 * hidden : 3 * hidden]) * proj[3 * hidden :]
            )
        send_a[u, :, :part, :] = lanes_l[...].reshape(n, part, tokens).astype(BF16)
        send_a[u, :, part:, :] = lanes_r[...].reshape(n, part, tokens).astype(BF16)
        if u == 0:
            pl.semaphore_wait(barrier, n - 1)
        start_all(bufs_a, u)
        recv_a[u, pl.ds(me, 1)] = send_a[u, pl.ds(me, 1)]
        for i in range(rows):
            gate[i] = sigmoid(jnp.dot(normed[i], w_gate_ref[u], preferred_element_type=F32))
        wait_all(bufs_a, u)
        dims = (((1,), (1,)), ((), ())) if u == 0 else (((0,), (0,)), ((), ()))
        for p in range(hb // 2):
            lo = 2 * p * rows
            lblk = recv_a[u, :, lo : lo + 2 * rows, :].astype(F32)
            rblk = recv_a[u, :, part + lo : part + lo + 2 * rows, :].astype(F32)
            for q in range(2):
                cut = slice(q * rows, (q + 1) * rows)
                lh = lblk[:, cut, :].reshape(n * rows, tokens).astype(BF16)
                rh = rblk[:, cut, :].reshape(n * rows, tokens).astype(BF16)
                tri = lax.dot_general(lh, rh, dims, preferred_element_type=F32)
                lanes_l[pl.ds(2 * p + q, n * rows, stride=hb), :] = tri
        send_b[u] = lanes_l[...].reshape(n, part, tokens).astype(BF16)
        start_all(bufs_b, u)
        recv_b[u, pl.ds(me, 1)] = send_b[u, pl.ds(me, 1)]
        wait_all(bufs_b, u)
        for p in range(rows // 2):
            lo = 2 * p * hb
            blk = recv_b[u, :, lo : lo + 2 * hb, :].astype(F32)
            for q in range(2):
                i = 2 * p + q
                tri = blk[:, q * hb : (q + 1) * hb, :].reshape(hidden, tokens).T
                mid = norm_lanes(
                    tri, gain_mid_ref[u : u + 1, :], bias_mid_ref[u : u + 1, :]
                ).astype(BF16)
                branch = jnp.dot(mid, w_out_ref[u], preferred_element_type=F32)
                new = (source[i].astype(F32) + gate[i] * branch).astype(BF16)
                if u == 0:
                    state[i] = new
                else:
                    out_ref[i] = new
                    mid_ref[i] = mid
    for u in range(2):
        drain(bufs_a, u)
        drain(bufs_b, u)


def fused(n, *operands):
    pair, hidden = operands[0], operands[3].shape[1]
    rows, tokens, channels = pair.shape
    part = hidden // n * rows
    vmem = pl.BlockSpec(memory_space=pltpu.VMEM)
    return pl.pallas_call(
        functools.partial(fused_kernel, n),
        out_shape=(
            jax.ShapeDtypeStruct(pair.shape, BF16),
            jax.ShapeDtypeStruct((rows, tokens, hidden), BF16),
        ),
        in_specs=[vmem] * len(operands),
        out_specs=(vmem, vmem),
        scratch_shapes=[
            pltpu.VMEM((2, 4 * hidden, channels), BF16),
            pltpu.VMEM(pair.shape, BF16),
            pltpu.VMEM(pair.shape, BF16),
            pltpu.VMEM(pair.shape, F32),
            pltpu.VMEM((hidden * rows, tokens), F32),
            pltpu.VMEM((hidden * rows, tokens), F32),
            pltpu.VMEM((2, n, 2 * part, tokens), BF16),
            pltpu.VMEM((2, n, 2 * part, tokens), BF16),
            pltpu.VMEM((2, n, part, tokens), BF16),
            pltpu.VMEM((2, n, part, tokens), BF16),
        ]
        + [pltpu.SemaphoreType.DMA((2, n))] * 4,
        compiler_params=pltpu.CompilerParams(
            collective_id=0, has_side_effects=True, vmem_limit_bytes=48 * 2**20
        ),
    )(*operands)


def fits(mesh, pair_shape, hidden):
    n = mesh.shape["row"]
    rows = pair_shape[0] // (n * mesh.shape["grp"])
    tokens = pair_shape[1]
    aligned = rows % 8 == 0 and hidden % (8 * n) == 0 and tokens % 128 == 0
    small = hidden * rows * tokens * 40 <= 40 * 2**20
    return mesh.shape["kc"] == 1 and n > 1 and n * rows == tokens and aligned and small


def solution(mesh):
    in_specs = (P(("grp", "row"), "kc", None), P(), P(), P(), P(), P(), P(), P())
    out_specs = (P(("grp", "row"), "kc", None), P(("grp", "row"), "kc", None))

    def run(*operands):
        if fits(mesh, operands[0].shape, operands[3].shape[1]):
            body = functools.partial(fused, mesh.shape["row"])
        else:
            body = shards
        return jax.shard_map(
            body, mesh=mesh, in_specs=in_specs, out_specs=out_specs, check_vma=False
        )(*operands)

    return run
```

```python
import functools

import jax
import jax.numpy as jnp
from jax import lax
from jax.experimental import pallas as pl
from jax.experimental.pallas import tpu as pltpu
from jax.sharding import PartitionSpec as P


def layer_norm(values, gain, bias, axis_pos):
    center = jnp.mean(values, axis=axis_pos, keepdims=True)
    spread = jnp.mean((values - center) ** 2, axis=axis_pos, keepdims=True)
    return (values - center) * lax.rsqrt(spread + 1e-05) * gain + bias


def prepare(state, layer_index, w_in, w_gate, gain_in, bias_in):
    hidden = w_in.shape[2] // 4
    pair_float = state.astype(jnp.float32)
    normed = layer_norm(pair_float, gain_in[layer_index], bias_in[layer_index], 2).astype(
        jnp.bfloat16
    )
    projected = jnp.einsum(
        "ijc,ch->hij", normed, w_in[layer_index], preferred_element_type=jnp.float32
    )
    left = (jax.nn.sigmoid(projected[:hidden]) * projected[hidden : 2 * hidden]).astype(
        jnp.bfloat16
    )
    right = (jax.nn.sigmoid(projected[2 * hidden : 3 * hidden]) * projected[3 * hidden :]).astype(
        jnp.bfloat16
    )
    gate_values = jax.nn.sigmoid(
        jnp.einsum("ijc,cd->ijd", normed, w_gate[layer_index], preferred_element_type=jnp.float32)
    )
    return (pair_float, left, right, gate_values)


def finish(pair_float, gate_values, returned, layer_index, w_out, gain_mid, bias_mid):
    middle = layer_norm(
        returned.astype(jnp.float32),
        gain_mid[layer_index][:, None],
        bias_mid[layer_index][:, None],
        1,
    ).astype(jnp.bfloat16)
    branch = jnp.einsum(
        "jhi,hc->ijc", middle, w_out[layer_index], preferred_element_type=jnp.float32
    )
    return ((pair_float + gate_values * branch).astype(jnp.bfloat16), middle)


def shards(pair, w_in, w_gate, w_out, gain_in, bias_in, gain_mid, bias_mid):
    pair_float, left, right, gate_values = prepare(pair, 0, w_in, w_gate, gain_in, bias_in)
    left_c, right_c = (
        lax.all_to_all(left, "row", split_axis=0, concat_axis=1, tiled=True),
        lax.all_to_all(right, "row", split_axis=0, concat_axis=1, tiled=True),
    )
    right_rows = right_c
    summed = lax.psum_scatter(
        jnp.einsum("hjs,his->jhi", right_rows, left_c, preferred_element_type=jnp.float32).astype(
            jnp.bfloat16
        ),
        "kc",
        scatter_dimension=0,
        tiled=True,
    ).astype(jnp.float32)
    returned = lax.all_to_all(
        summed.astype(jnp.bfloat16), "row", split_axis=2, concat_axis=1, tiled=True
    )
    state, unused = finish(pair_float, gate_values, returned, 0, w_out, gain_mid, bias_mid)
    pair_float, left, right, gate_values = prepare(state, 1, w_in, w_gate, gain_in, bias_in)
    left_c, right_c = (
        lax.all_to_all(left, "row", split_axis=0, concat_axis=1, tiled=True),
        lax.all_to_all(right, "row", split_axis=0, concat_axis=1, tiled=True),
    )
    summed = jnp.einsum(
        "hpj,hpi->jhi",
        right_c,
        lax.all_gather(left_c, "kc", axis=2, tiled=True),
        preferred_element_type=jnp.float32,
    )
    returned = lax.all_to_all(
        summed.astype(jnp.bfloat16), "row", split_axis=2, concat_axis=1, tiled=True
    )
    final_state, middle = finish(pair_float, gate_values, returned, 1, w_out, gain_mid, bias_mid)
    return (final_state, middle.transpose(2, 0, 1))

MESH = pl.DeviceIdType.MESH
F32 = jnp.float32
BF16 = jnp.bfloat16
CHUNKS = 1
VMEM_BYTES = 64 * 2**20 - 2**16


def sigmoid(x):
    return 0.5 * jnp.tanh(0.5 * x) + 0.5


def norm_lanes(x, gain, bias):
    center = jnp.mean(x, axis=-1, keepdims=True)
    moved = x - center
    spread = jnp.mean(moved * moved, axis=-1, keepdims=True)
    return moved * lax.rsqrt(spread + 1e-05) * gain + bias


def fused_kernel(
    n,
    chunks,
    *refs,
):
    operands, refs = refs[:8], refs[8:]
    out_ref, mid_ref = refs[:2]
    loaded, refs = refs[2:10], refs[10:]
    (
        load_sem,
        w_t,
        state,
        normed,
        gate,
        lanes_l,
        lanes_r,
        send_a,
        recv_a,
        send_b,
        recv_b,
        sa_sem,
        ra_sem,
        sb_sem,
        rb_sem,
    ) = refs
    loads = [
        pltpu.make_async_copy(src, dst, load_sem.at[k])
        for k, (src, dst) in enumerate(zip(operands, loaded))
    ]
    for load in loads:
        load.start()
    (
        pair_ref,
        w_in_ref,
        w_gate_ref,
        w_out_ref,
        gain_in_ref,
        bias_in_ref,
        gain_mid_ref,
        bias_mid_ref,
    ) = loaded
    rows, tokens, channels = pair_ref.shape
    hidden = w_out_ref.shape[1]
    hb = hidden // n
    part = hb * rows
    per = hb // chunks
    piece = per * rows
    me = lax.axis_index("row")

    barrier = pltpu.get_barrier_semaphore()

    def greet(o, c):
        pl.semaphore_signal(
            barrier, inc=1, device_id={"row": lax.rem(me + o, n)}, device_id_type=MESH
        )
        return c

    lax.fori_loop(1, n, greet, 0)

    def start_all(bufs, k):
        send, recv, ssem, rsem = bufs

        def body(o, c):
            other = lax.rem(me + o, n)
            pltpu.make_async_remote_copy(
                src_ref=send.at[k, other],
                dst_ref=recv.at[k, me],
                send_sem=ssem.at[k],
                recv_sem=rsem.at[k],
                device_id={"row": other},
                device_id_type=MESH,
            ).start()
            return c

        lax.fori_loop(1, n, body, 0)

    def wait_all(bufs, k):
        send, recv, ssem, rsem = bufs
        blocks = recv.at[k, pl.ds(0, n - 1)]
        pltpu.make_async_copy(blocks, blocks, rsem.at[k]).wait()

    def drain(bufs, k):
        send, recv, ssem, rsem = bufs
        blocks = send.at[k, pl.ds(0, n - 1)]
        pltpu.make_async_copy(blocks, blocks, ssem.at[k]).wait()

    bufs_a = (send_a, recv_a, sa_sem, ra_sem)
    bufs_b = (send_b, recv_b, sb_sem, rb_sem)

    for k in (1, 4, 5, 0):
        loads[k].wait()
    w_t[0] = w_in_ref[0].T

    for u in range(2):
        source = pair_ref if u == 0 else state
        for i in range(rows):
            x = source[i].astype(F32)
            nrm = norm_lanes(x, gain_in_ref[u : u + 1, :], bias_in_ref[u : u + 1, :]).astype(BF16)
            normed[i] = nrm
            proj = lax.dot_general(
                w_t[u], nrm, (((1,), (1,)), ((), ())), preferred_element_type=F32
            )
            lanes_l[pl.ds(i, hidden, stride=rows), :] = (
                sigmoid(proj[:hidden]) * proj[hidden : 2 * hidden]
            )
            lanes_r[pl.ds(i, hidden, stride=rows), :] = (
                sigmoid(proj[2 * hidden : 3 * hidden]) * proj[3 * hidden :]
            )
        if u == 0:
            pl.semaphore_wait(barrier, n - 1)
        left = lanes_l[...].reshape(n, part, tokens)
        right = lanes_r[...].reshape(n, part, tokens)
        for c in range(chunks):
            own = slice(c * piece, (c + 1) * piece)
            send_a[u * chunks + c, :, :piece, :] = left[:, own].astype(BF16)
            send_a[u * chunks + c, :, piece:, :] = right[:, own].astype(BF16)
            start_all(bufs_a, u * chunks + c)
        for c in range(chunks):
            k = u * chunks + c
            recv_a[k, pl.ds(me, 1)] = send_a[k, pl.ds(me, 1)]
        if u == 0:
            w_t[1] = w_in_ref[1].T
            for k in (2, 3, 6, 7):
                loads[k].wait()
        for i in range(rows):
            gate[i] = sigmoid(jnp.dot(normed[i], w_gate_ref[u], preferred_element_type=F32))
        dims = (((1,), (1,)), ((), ())) if u == 0 else (((0,), (0,)), ((), ()))
        for c in range(chunks):
            k = u * chunks + c
            wait_all(bufs_a, k)
            for p in range(per // 2):
                pair_of = slice(2 * p * rows, 2 * (p + 1) * rows)
                lblk = recv_a[k, :, pair_of, :].astype(F32)
                rblk = recv_a[k, :, piece + 2 * p * rows : piece + 2 * (p + 1) * rows, :].astype(F32)
                tri = []
                for q in range(2):
                    cut = slice(q * rows, (q + 1) * rows)
                    lh = lblk[:, cut, :].reshape(n * rows, tokens).astype(BF16)
                    rh = rblk[:, cut, :].reshape(n * rows, tokens).astype(BF16)
                    one = lax.dot_general(lh, rh, dims, preferred_element_type=F32)
                    tri.append(one.reshape(n, rows, tokens))
                send_b[k, :, pair_of, :] = jnp.concatenate(tri, axis=1).astype(BF16)
            start_all(bufs_b, k)
            recv_b[k, pl.ds(me, 1)] = send_b[k, pl.ds(me, 1)]
        for c in range(chunks):
            k = u * chunks + c
            drain(bufs_a, k)
            wait_all(bufs_b, k)
            for d in range(n):
                at = d * part + c * piece
                lanes_l[at : at + piece, :] = recv_b[k, d].astype(F32)
        for i in range(rows):
            tri = lanes_l[pl.ds(i, hidden, stride=rows), :].T
            mid = norm_lanes(
                tri, gain_mid_ref[u : u + 1, :], bias_mid_ref[u : u + 1, :]
            ).astype(BF16)
            branch = jnp.dot(mid, w_out_ref[u], preferred_element_type=F32)
            new = (source[i].astype(F32) + gate[i] * branch).astype(BF16)
            if u == 0:
                state[i] = new
            else:
                out_ref[i] = new
                mid_ref[i] = mid
    for k in range(2 * chunks):
        drain(bufs_b, k)


def fused(n, *operands):
    pair, hidden = operands[0], operands[3].shape[1]
    rows, tokens, channels = pair.shape
    chunks = CHUNKS if hidden // n % (2 * CHUNKS) == 0 else 1
    piece = hidden // n * rows // chunks
    vmem = pl.BlockSpec(memory_space=pltpu.VMEM)
    return pl.pallas_call(
        functools.partial(fused_kernel, n, chunks),
        out_shape=(
            jax.ShapeDtypeStruct(pair.shape, BF16),
            jax.ShapeDtypeStruct((rows, tokens, hidden), BF16),
        ),
        in_specs=[pl.BlockSpec(memory_space=pltpu.HBM)] * len(operands),
        out_specs=(vmem, vmem),
        scratch_shapes=[pltpu.VMEM(operand.shape, operand.dtype) for operand in operands]
        + [
            pltpu.SemaphoreType.DMA((len(operands),)),
            pltpu.VMEM((2, 4 * hidden, channels), BF16),
            pltpu.VMEM(pair.shape, BF16),
            pltpu.VMEM(pair.shape, BF16),
            pltpu.VMEM(pair.shape, F32),
            pltpu.VMEM((hidden * rows, tokens), F32),
            pltpu.VMEM((hidden * rows, tokens), F32),
            pltpu.VMEM((2 * chunks, n, 2 * piece, tokens), BF16),
            pltpu.VMEM((2 * chunks, n, 2 * piece, tokens), BF16),
            pltpu.VMEM((2 * chunks, n, piece, tokens), BF16),
            pltpu.VMEM((2 * chunks, n, piece, tokens), BF16),
        ]
        + [pltpu.SemaphoreType.DMA((2 * chunks,))] * 4,
        compiler_params=pltpu.CompilerParams(
            collective_id=0, has_side_effects=True, vmem_limit_bytes=VMEM_BYTES
        ),
    )(*operands)


def fits(mesh, pair_shape, hidden):
    n = mesh.shape["row"]
    rows = pair_shape[0] // (n * mesh.shape["grp"])
    tokens = pair_shape[1]
    aligned = rows % 8 == 0 and hidden % (8 * n) == 0 and tokens % 128 == 0
    small = hidden * rows * tokens * 40 <= 40 * 2**20
    return mesh.shape["kc"] == 1 and n > 1 and n * rows == tokens and aligned and small


def solution(mesh):
    in_specs = (P(("grp", "row"), "kc", None), P(), P(), P(), P(), P(), P(), P())
    out_specs = (P(("grp", "row"), "kc", None), P(("grp", "row"), "kc", None))

    def run(*operands):
        if fits(mesh, operands[0].shape, operands[3].shape[1]):
            body = functools.partial(fused, mesh.shape["row"])
        else:
            body = shards
        return jax.shard_map(
            body, mesh=mesh, in_specs=in_specs, out_specs=out_specs, check_vma=False
        )(*operands)

    return run
```

```python
import functools

import jax
import jax.numpy as jnp
from jax import lax
from jax.experimental import pallas as pl
from jax.experimental.pallas import tpu as pltpu
from jax.sharding import PartitionSpec as P


def layer_norm(values, gain, bias, axis_pos):
    center = jnp.mean(values, axis=axis_pos, keepdims=True)
    spread = jnp.mean((values - center) ** 2, axis=axis_pos, keepdims=True)
    return (values - center) * lax.rsqrt(spread + 1e-05) * gain + bias


def prepare(state, layer_index, w_in, w_gate, gain_in, bias_in):
    hidden = w_in.shape[2] // 4
    pair_float = state.astype(jnp.float32)
    normed = layer_norm(pair_float, gain_in[layer_index], bias_in[layer_index], 2).astype(
        jnp.bfloat16
    )
    projected = jnp.einsum(
        "ijc,ch->hij", normed, w_in[layer_index], preferred_element_type=jnp.float32
    )
    left = (jax.nn.sigmoid(projected[:hidden]) * projected[hidden : 2 * hidden]).astype(
        jnp.bfloat16
    )
    right = (jax.nn.sigmoid(projected[2 * hidden : 3 * hidden]) * projected[3 * hidden :]).astype(
        jnp.bfloat16
    )
    gate_values = jax.nn.sigmoid(
        jnp.einsum("ijc,cd->ijd", normed, w_gate[layer_index], preferred_element_type=jnp.float32)
    )
    return (pair_float, left, right, gate_values)


def finish(pair_float, gate_values, returned, layer_index, w_out, gain_mid, bias_mid):
    middle = layer_norm(
        returned.astype(jnp.float32),
        gain_mid[layer_index][:, None],
        bias_mid[layer_index][:, None],
        1,
    ).astype(jnp.bfloat16)
    branch = jnp.einsum(
        "jhi,hc->ijc", middle, w_out[layer_index], preferred_element_type=jnp.float32
    )
    return ((pair_float + gate_values * branch).astype(jnp.bfloat16), middle)


def shards(pair, w_in, w_gate, w_out, gain_in, bias_in, gain_mid, bias_mid):
    pair_float, left, right, gate_values = prepare(pair, 0, w_in, w_gate, gain_in, bias_in)
    left_c, right_c = (
        lax.all_to_all(left, "row", split_axis=0, concat_axis=1, tiled=True),
        lax.all_to_all(right, "row", split_axis=0, concat_axis=1, tiled=True),
    )
    right_rows = right_c
    summed = lax.psum_scatter(
        jnp.einsum("hjs,his->jhi", right_rows, left_c, preferred_element_type=jnp.float32).astype(
            jnp.bfloat16
        ),
        "kc",
        scatter_dimension=0,
        tiled=True,
    ).astype(jnp.float32)
    returned = lax.all_to_all(
        summed.astype(jnp.bfloat16), "row", split_axis=2, concat_axis=1, tiled=True
    )
    state, unused = finish(pair_float, gate_values, returned, 0, w_out, gain_mid, bias_mid)
    pair_float, left, right, gate_values = prepare(state, 1, w_in, w_gate, gain_in, bias_in)
    left_c, right_c = (
        lax.all_to_all(left, "row", split_axis=0, concat_axis=1, tiled=True),
        lax.all_to_all(right, "row", split_axis=0, concat_axis=1, tiled=True),
    )
    summed = jnp.einsum(
        "hpj,hpi->jhi",
        right_c,
        lax.all_gather(left_c, "kc", axis=2, tiled=True),
        preferred_element_type=jnp.float32,
    )
    returned = lax.all_to_all(
        summed.astype(jnp.bfloat16), "row", split_axis=2, concat_axis=1, tiled=True
    )
    final_state, middle = finish(pair_float, gate_values, returned, 1, w_out, gain_mid, bias_mid)
    return (final_state, middle.transpose(2, 0, 1))

MESH = pl.DeviceIdType.MESH
F32 = jnp.float32
BF16 = jnp.bfloat16
CHUNKS = 1
VMEM_BYTES = 64 * 2**20 - 2**16


def sigmoid(x):
    return 0.5 * jnp.tanh(0.5 * x) + 0.5


def norm_lanes(x, gain, bias):
    center = jnp.mean(x, axis=-1, keepdims=True)
    moved = x - center
    spread = jnp.mean(moved * moved, axis=-1, keepdims=True)
    return moved * lax.rsqrt(spread + 1e-05) * gain + bias


def fused_kernel(
    n,
    chunks,
    *refs,
):
    operands, refs = refs[:8], refs[8:]
    out_ref, mid_ref = refs[:2]
    loaded, refs = refs[2:10], refs[10:]
    (
        load_sem,
        w_t,
        state,
        normed,
        gate,
        lanes_l,
        lanes_r,
        send_a,
        recv_a,
        send_b,
        recv_b,
        sa_sem,
        ra_sem,
        sb_sem,
        rb_sem,
    ) = refs
    loads = [
        pltpu.make_async_copy(src, dst, load_sem.at[k])
        for k, (src, dst) in enumerate(zip(operands, loaded))
    ]
    for load in loads:
        load.start()
    (
        pair_ref,
        w_in_ref,
        w_gate_ref,
        w_out_ref,
        gain_in_ref,
        bias_in_ref,
        gain_mid_ref,
        bias_mid_ref,
    ) = loaded
    rows, tokens, channels = pair_ref.shape
    hidden = w_out_ref.shape[1]
    hb = hidden // n
    part = hb * rows
    per = hb // chunks
    piece = per * rows
    me = lax.axis_index("row")

    barrier = pltpu.get_barrier_semaphore()

    def greet(o, c):
        pl.semaphore_signal(
            barrier, inc=1, device_id={"row": lax.rem(me + o, n)}, device_id_type=MESH
        )
        return c

    lax.fori_loop(1, n, greet, 0)

    flips = []
    for bit in range(n.bit_length() - 1):
        size = 2**bit
        flips.append(size - 2 * size * lax.rem(lax.div(me, size), 2))

    def start_all(bufs, k, offsets):
        send, recv, ssem, rsem = bufs
        for o in offsets:
            other = me
            for bit, flip in enumerate(flips):
                if o // 2**bit % 2 == 1:
                    other = other + flip
            pltpu.make_async_remote_copy(
                src_ref=send.at[k, other],
                dst_ref=recv.at[k, me],
                send_sem=ssem.at[k],
                recv_sem=rsem.at[k],
                device_id={"row": other},
                device_id_type=MESH,
            ).start()

    def wait_all(bufs, k):
        send, recv, ssem, rsem = bufs
        blocks = recv.at[k, pl.ds(0, n - 1)]
        pltpu.make_async_copy(blocks, blocks, rsem.at[k]).wait()

    def drain(bufs, k):
        send, recv, ssem, rsem = bufs
        blocks = send.at[k, pl.ds(0, n - 1)]
        pltpu.make_async_copy(blocks, blocks, ssem.at[k]).wait()

    bufs_a = (send_a, recv_a, sa_sem, ra_sem)
    bufs_b = (send_b, recv_b, sb_sem, rb_sem)

    for k in (1, 4, 5, 0):
        loads[k].wait()
    w_t[0] = w_in_ref[0].T

    for u in range(2):
        source = pair_ref if u == 0 else state
        for i in range(rows):
            x = source[i].astype(F32)
            normed[i] = norm_lanes(
                x, gain_in_ref[u : u + 1, :], bias_in_ref[u : u + 1, :]
            ).astype(BF16)
        half, wide = n // 2, hidden // 2
        own_half = lax.div(me, half)
        for stage, side in enumerate((1 - own_half, own_half)):
            first = pl.multiple_of(side * wide, wide)
            weights = jnp.concatenate(
                [w_t[u, pl.ds(g * hidden + first, wide), :] for g in range(4)], axis=0
            )
            base = stage * wide * rows
            for i in range(rows):
                proj = lax.dot_general(
                    weights, normed[i], (((1,), (1,)), ((), ())), preferred_element_type=F32
                )
                at = pl.ds(base + i, wide, stride=rows)
                lanes_l[at, :] = sigmoid(proj[:wide]) * proj[wide : 2 * wide]
                lanes_r[at, :] = sigmoid(proj[2 * wide : 3 * wide]) * proj[3 * wide :]
            owners = pl.ds(side * half, half)
            part_of = slice(base, base + wide * rows)
            left = lanes_l[part_of, :].reshape(half, part, tokens)
            right = lanes_r[part_of, :].reshape(half, part, tokens)
            send_a[u, owners, :part, :] = left.astype(BF16)
            send_a[u, owners, part:, :] = right.astype(BF16)
            if u == 0 and stage == 0:
                pl.semaphore_wait(barrier, n - 1)
            start_all(bufs_a, u, range(n - 1, half - 1, -1) if stage == 0 else range(half - 1, 0, -1))
        for c in range(chunks):
            k = u * chunks + c
            recv_a[k, pl.ds(me, 1)] = send_a[k, pl.ds(me, 1)]
        if u == 0:
            w_t[1] = w_in_ref[1].T
            for k in (2, 3, 6, 7):
                loads[k].wait()
        for i in range(rows):
            gate[i] = sigmoid(jnp.dot(normed[i], w_gate_ref[u], preferred_element_type=F32))
        dims = (((1,), (1,)), ((), ())) if u == 0 else (((0,), (0,)), ((), ()))
        for c in range(chunks):
            k = u * chunks + c
            wait_all(bufs_a, k)
            for p in range(per // 2):
                pair_of = slice(2 * p * rows, 2 * (p + 1) * rows)
                lblk = recv_a[k, :, pair_of, :].astype(F32)
                rblk = recv_a[k, :, piece + 2 * p * rows : piece + 2 * (p + 1) * rows, :].astype(F32)
                tri = []
                for q in range(2):
                    cut = slice(q * rows, (q + 1) * rows)
                    lh = lblk[:, cut, :].reshape(n * rows, tokens).astype(BF16)
                    rh = rblk[:, cut, :].reshape(n * rows, tokens).astype(BF16)
                    one = lax.dot_general(lh, rh, dims, preferred_element_type=F32)
                    tri.append(one.reshape(n, rows, tokens))
                send_b[k, :, pair_of, :] = jnp.concatenate(tri, axis=1).astype(BF16)
            start_all(bufs_b, k, range(n - 1, 0, -1))
            recv_b[k, pl.ds(me, 1)] = send_b[k, pl.ds(me, 1)]
        for c in range(chunks):
            k = u * chunks + c
            drain(bufs_a, k)
            wait_all(bufs_b, k)
            for d in range(n):
                at = d * part + c * piece
                lanes_l[at : at + piece, :] = recv_b[k, d].astype(F32)
        for i in range(rows):
            tri = lanes_l[pl.ds(i, hidden, stride=rows), :].T
            mid = norm_lanes(
                tri, gain_mid_ref[u : u + 1, :], bias_mid_ref[u : u + 1, :]
            ).astype(BF16)
            branch = jnp.dot(mid, w_out_ref[u], preferred_element_type=F32)
            new = (source[i].astype(F32) + gate[i] * branch).astype(BF16)
            if u == 0:
                state[i] = new
            else:
                out_ref[i] = new
                mid_ref[i] = mid
    for k in range(2 * chunks):
        drain(bufs_b, k)


def fused(n, *operands):
    pair, hidden = operands[0], operands[3].shape[1]
    rows, tokens, channels = pair.shape
    chunks = CHUNKS if hidden // n % (2 * CHUNKS) == 0 else 1
    piece = hidden // n * rows // chunks
    vmem = pl.BlockSpec(memory_space=pltpu.VMEM)
    return pl.pallas_call(
        functools.partial(fused_kernel, n, chunks),
        out_shape=(
            jax.ShapeDtypeStruct(pair.shape, BF16),
            jax.ShapeDtypeStruct((rows, tokens, hidden), BF16),
        ),
        in_specs=[pl.BlockSpec(memory_space=pltpu.HBM)] * len(operands),
        out_specs=(vmem, vmem),
        scratch_shapes=[pltpu.VMEM(operand.shape, operand.dtype) for operand in operands]
        + [
            pltpu.SemaphoreType.DMA((len(operands),)),
            pltpu.VMEM((2, 4 * hidden, channels), BF16),
            pltpu.VMEM(pair.shape, BF16),
            pltpu.VMEM(pair.shape, BF16),
            pltpu.VMEM(pair.shape, F32),
            pltpu.VMEM((hidden * rows, tokens), F32),
            pltpu.VMEM((hidden * rows, tokens), F32),
            pltpu.VMEM((2 * chunks, n, 2 * piece, tokens), BF16),
            pltpu.VMEM((2 * chunks, n, 2 * piece, tokens), BF16),
            pltpu.VMEM((2 * chunks, n, piece, tokens), BF16),
            pltpu.VMEM((2 * chunks, n, piece, tokens), BF16),
        ]
        + [pltpu.SemaphoreType.DMA((2 * chunks,))] * 4,
        compiler_params=pltpu.CompilerParams(
            collective_id=0, has_side_effects=True, vmem_limit_bytes=VMEM_BYTES
        ),
    )(*operands)


def fits(mesh, pair_shape, hidden):
    n = mesh.shape["row"]
    rows = pair_shape[0] // (n * mesh.shape["grp"])
    tokens = pair_shape[1]
    aligned = rows % 8 == 0 and hidden % (8 * n) == 0 and tokens % 128 == 0
    small = hidden * rows * tokens * 40 <= 40 * 2**20
    return mesh.shape["kc"] == 1 and n > 1 and n & (n - 1) == 0 and n * rows == tokens and aligned and small


def solution(mesh):
    in_specs = (P(("grp", "row"), "kc", None), P(), P(), P(), P(), P(), P(), P())
    out_specs = (P(("grp", "row"), "kc", None), P(("grp", "row"), "kc", None))

    def run(*operands):
        if fits(mesh, operands[0].shape, operands[3].shape[1]):
            body = functools.partial(fused, mesh.shape["row"])
        else:
            body = shards
        return jax.shard_map(
            body, mesh=mesh, in_specs=in_specs, out_specs=out_specs, check_vma=False
        )(*operands)

    return run
```

```python
import functools

import jax
import jax.numpy as jnp
from jax import lax
from jax.experimental import pallas as pl
from jax.experimental.pallas import tpu as pltpu
from jax.sharding import PartitionSpec as P


def layer_norm(values, gain, bias, axis_pos):
    center = jnp.mean(values, axis=axis_pos, keepdims=True)
    spread = jnp.mean((values - center) ** 2, axis=axis_pos, keepdims=True)
    return (values - center) * lax.rsqrt(spread + 1e-05) * gain + bias


def prepare(state, layer_index, w_in, w_gate, gain_in, bias_in):
    hidden = w_in.shape[2] // 4
    pair_float = state.astype(jnp.float32)
    normed = layer_norm(pair_float, gain_in[layer_index], bias_in[layer_index], 2).astype(
        jnp.bfloat16
    )
    projected = jnp.einsum(
        "ijc,ch->hij", normed, w_in[layer_index], preferred_element_type=jnp.float32
    )
    left = (jax.nn.sigmoid(projected[:hidden]) * projected[hidden : 2 * hidden]).astype(
        jnp.bfloat16
    )
    right = (jax.nn.sigmoid(projected[2 * hidden : 3 * hidden]) * projected[3 * hidden :]).astype(
        jnp.bfloat16
    )
    gate_values = jax.nn.sigmoid(
        jnp.einsum("ijc,cd->ijd", normed, w_gate[layer_index], preferred_element_type=jnp.float32)
    )
    return (pair_float, left, right, gate_values)


def finish(pair_float, gate_values, returned, layer_index, w_out, gain_mid, bias_mid):
    middle = layer_norm(
        returned.astype(jnp.float32),
        gain_mid[layer_index][:, None],
        bias_mid[layer_index][:, None],
        1,
    ).astype(jnp.bfloat16)
    branch = jnp.einsum(
        "jhi,hc->ijc", middle, w_out[layer_index], preferred_element_type=jnp.float32
    )
    return ((pair_float + gate_values * branch).astype(jnp.bfloat16), middle)


def shards(pair, w_in, w_gate, w_out, gain_in, bias_in, gain_mid, bias_mid):
    pair_float, left, right, gate_values = prepare(pair, 0, w_in, w_gate, gain_in, bias_in)
    left_c, right_c = (
        lax.all_to_all(left, "row", split_axis=0, concat_axis=1, tiled=True),
        lax.all_to_all(right, "row", split_axis=0, concat_axis=1, tiled=True),
    )
    right_rows = right_c
    summed = lax.psum_scatter(
        jnp.einsum("hjs,his->jhi", right_rows, left_c, preferred_element_type=jnp.float32).astype(
            jnp.bfloat16
        ),
        "kc",
        scatter_dimension=0,
        tiled=True,
    ).astype(jnp.float32)
    returned = lax.all_to_all(
        summed.astype(jnp.bfloat16), "row", split_axis=2, concat_axis=1, tiled=True
    )
    state, unused = finish(pair_float, gate_values, returned, 0, w_out, gain_mid, bias_mid)
    pair_float, left, right, gate_values = prepare(state, 1, w_in, w_gate, gain_in, bias_in)
    left_c, right_c = (
        lax.all_to_all(left, "row", split_axis=0, concat_axis=1, tiled=True),
        lax.all_to_all(right, "row", split_axis=0, concat_axis=1, tiled=True),
    )
    summed = jnp.einsum(
        "hpj,hpi->jhi",
        right_c,
        lax.all_gather(left_c, "kc", axis=2, tiled=True),
        preferred_element_type=jnp.float32,
    )
    returned = lax.all_to_all(
        summed.astype(jnp.bfloat16), "row", split_axis=2, concat_axis=1, tiled=True
    )
    final_state, middle = finish(pair_float, gate_values, returned, 1, w_out, gain_mid, bias_mid)
    return (final_state, middle.transpose(2, 0, 1))

MESH = pl.DeviceIdType.MESH
F32 = jnp.float32
BF16 = jnp.bfloat16
CHUNKS = 1
VMEM_BYTES = 64 * 2**20 - 2**16


def sigmoid(x):
    return 0.5 * jnp.tanh(0.5 * x) + 0.5


def norm_lanes(x, gain, bias):
    center = jnp.mean(x, axis=-1, keepdims=True)
    moved = x - center
    spread = jnp.mean(moved * moved, axis=-1, keepdims=True)
    return moved * lax.rsqrt(spread + 1e-05) * gain + bias


def fused_kernel(
    n,
    chunks,
    *refs,
):
    operands, refs = refs[:8], refs[8:]
    out_ref, mid_ref = refs[:2]
    loaded, refs = refs[2:10], refs[10:]
    (
        load_sem,
        w_t,
        state,
        normed,
        gate,
        lanes_l,
        lanes_r,
        send_a,
        recv_a,
        send_b,
        recv_b,
        sa_sem,
        ra_sem,
        sb_sem,
        rb_sem,
    ) = refs
    loads = [
        pltpu.make_async_copy(src, dst, load_sem.at[k])
        for k, (src, dst) in enumerate(zip(operands, loaded))
    ]
    for load in loads:
        load.start()
    (
        pair_ref,
        w_in_ref,
        w_gate_ref,
        w_out_ref,
        gain_in_ref,
        bias_in_ref,
        gain_mid_ref,
        bias_mid_ref,
    ) = loaded
    rows, tokens, channels = pair_ref.shape
    hidden = w_out_ref.shape[1]
    hb = hidden // n
    part = hb * rows
    per = hb // chunks
    piece = per * rows
    me = lax.axis_index("row")

    barrier = pltpu.get_barrier_semaphore()

    def greet(o, c):
        pl.semaphore_signal(
            barrier, inc=1, device_id={"row": lax.rem(me + o, n)}, device_id_type=MESH
        )
        return c

    lax.fori_loop(1, n, greet, 0)

    flips = []
    for bit in range(n.bit_length() - 1):
        size = 2**bit
        flips.append(size - 2 * size * lax.rem(lax.div(me, size), 2))

    def start_all(bufs, k, offsets):
        send, recv, ssem, rsem = bufs
        for o in offsets:
            other = me
            for bit, flip in enumerate(flips):
                if o // 2**bit % 2 == 1:
                    other = other + flip
            pltpu.make_async_remote_copy(
                src_ref=send.at[k, other],
                dst_ref=recv.at[k, me],
                send_sem=ssem.at[k],
                recv_sem=rsem.at[k],
                device_id={"row": other},
                device_id_type=MESH,
            ).start()

    def wait_all(bufs, k):
        send, recv, ssem, rsem = bufs
        blocks = recv.at[k, pl.ds(0, n - 1)]
        pltpu.make_async_copy(blocks, blocks, rsem.at[k]).wait()

    def drain(bufs, k):
        send, recv, ssem, rsem = bufs
        blocks = send.at[k, pl.ds(0, n - 1)]
        pltpu.make_async_copy(blocks, blocks, ssem.at[k]).wait()

    bufs_a = (send_a, recv_a, sa_sem, ra_sem)
    bufs_b = (send_b, recv_b, sb_sem, rb_sem)

    for k in (1, 4, 5, 0):
        loads[k].wait()
    w_t[0] = w_in_ref[0].T

    for u in range(2):
        source = pair_ref if u == 0 else state
        for i in range(rows):
            x = source[i].astype(F32)
            normed[i] = norm_lanes(
                x, gain_in_ref[u : u + 1, :], bias_in_ref[u : u + 1, :]
            ).astype(BF16)
        half, wide = n // 2, hidden // 2
        own_half = lax.div(me, half)
        for stage, side in enumerate((1 - own_half, own_half)):
            first = pl.multiple_of(side * wide, wide)
            weights = jnp.concatenate(
                [w_t[u, pl.ds(g * hidden + first, wide), :] for g in range(4)], axis=0
            )
            base = stage * wide * rows
            for i in range(rows):
                proj = lax.dot_general(
                    weights, normed[i], (((1,), (1,)), ((), ())), preferred_element_type=F32
                )
                at = pl.ds(base + i, wide, stride=rows)
                lanes_l[at, :] = sigmoid(proj[:wide]) * proj[wide : 2 * wide]
                lanes_r[at, :] = sigmoid(proj[2 * wide : 3 * wide]) * proj[3 * wide :]
            owners = pl.ds(side * half, half)
            part_of = slice(base, base + wide * rows)
            left = lanes_l[part_of, :].reshape(half, part, tokens)
            right = lanes_r[part_of, :].reshape(half, part, tokens)
            send_a[u, owners, :part, :] = left.astype(BF16)
            send_a[u, owners, part:, :] = right.astype(BF16)
            if u == 0 and stage == 0:
                pl.semaphore_wait(barrier, n - 1)
            start_all(bufs_a, u, range(n - 1, half - 1, -1) if stage == 0 else range(half - 1, 0, -1))
        for c in range(chunks):
            k = u * chunks + c
            recv_a[k, pl.ds(me, 1)] = send_a[k, pl.ds(me, 1)]
        if u == 0:
            w_t[1] = w_in_ref[1].T
            for k in (2, 3, 6, 7):
                loads[k].wait()
        for i in range(rows):
            gate[i] = sigmoid(jnp.dot(normed[i], w_gate_ref[u], preferred_element_type=F32))
        dims = (((1,), (1,)), ((), ())) if u == 0 else (((0,), (0,)), ((), ()))
        for c in range(chunks):
            k = u * chunks + c
            wait_all(bufs_a, k)
            for p in range(per // 2):
                pair_of = slice(2 * p * rows, 2 * (p + 1) * rows)
                lblk = recv_a[k, :, pair_of, :].astype(F32)
                rblk = recv_a[k, :, piece + 2 * p * rows : piece + 2 * (p + 1) * rows, :].astype(F32)
                tri = []
                for q in range(2):
                    cut = slice(q * rows, (q + 1) * rows)
                    lh = lblk[:, cut, :].reshape(n * rows, tokens).astype(BF16)
                    rh = rblk[:, cut, :].reshape(n * rows, tokens).astype(BF16)
                    one = lax.dot_general(lh, rh, dims, preferred_element_type=F32)
                    tri.append(one.reshape(n, rows, tokens))
                send_b[k, :, pair_of, :] = jnp.concatenate(tri, axis=1).astype(BF16)
            start_all(bufs_b, k, range(n - 1, 0, -1))
            recv_b[k, pl.ds(me, 1)] = send_b[k, pl.ds(me, 1)]
        for c in range(chunks):
            k = u * chunks + c
            drain(bufs_a, k)
            wait_all(bufs_b, k)
            for d in range(n):
                at = d * part + c * piece
                lanes_l[at : at + piece, :] = recv_b[k, d].astype(F32)
        for i in range(rows):
            tri = lanes_l[pl.ds(i, hidden, stride=rows), :].T
            mid = norm_lanes(
                tri, gain_mid_ref[u : u + 1, :], bias_mid_ref[u : u + 1, :]
            ).astype(BF16)
            branch = jnp.dot(mid, w_out_ref[u], preferred_element_type=F32)
            new = (source[i].astype(F32) + gate[i] * branch).astype(BF16)
            if u == 0:
                state[i] = new
            else:
                out_ref[i] = new
                mid_ref[i] = mid
    for k in range(2 * chunks):
        drain(bufs_b, k)


def fused(n, *operands):
    pair, hidden = operands[0], operands[3].shape[1]
    rows, tokens, channels = pair.shape
    chunks = CHUNKS if hidden // n % (2 * CHUNKS) == 0 else 1
    piece = hidden // n * rows // chunks
    vmem = pl.BlockSpec(memory_space=pltpu.VMEM)
    return pl.pallas_call(
        functools.partial(fused_kernel, n, chunks),
        out_shape=(
            jax.ShapeDtypeStruct(pair.shape, BF16),
            jax.ShapeDtypeStruct((rows, tokens, hidden), BF16),
        ),
        in_specs=[pl.BlockSpec(memory_space=pltpu.HBM)] * len(operands),
        out_specs=(vmem, vmem),
        scratch_shapes=[pltpu.VMEM(operand.shape, operand.dtype) for operand in operands]
        + [
            pltpu.SemaphoreType.DMA((len(operands),)),
            pltpu.VMEM((2, 4 * hidden, channels), BF16),
            pltpu.VMEM(pair.shape, BF16),
            pltpu.VMEM(pair.shape, BF16),
            pltpu.VMEM(pair.shape, F32),
            pltpu.VMEM((hidden * rows, tokens), F32),
            pltpu.VMEM((hidden * rows, tokens), F32),
            pltpu.VMEM((2 * chunks, n, 2 * piece, tokens), BF16),
            pltpu.VMEM((2 * chunks, n, 2 * piece, tokens), BF16),
            pltpu.VMEM((2 * chunks, n, piece, tokens), BF16),
            pltpu.VMEM((2 * chunks, n, piece, tokens), BF16),
        ]
        + [pltpu.SemaphoreType.DMA((2 * chunks,))] * 4,
        compiler_params=pltpu.CompilerParams(
            collective_id=0, has_side_effects=True, vmem_limit_bytes=VMEM_BYTES
        ),
    )(*operands)


def store_kernel(new_ref, mid_ref, out_ref, out_mid_ref, held, sem_in, sem_out):
    pieces = held.shape[1]
    moves = []
    for which, (src, dst) in enumerate(((new_ref, out_ref), (mid_ref, out_mid_ref))):
        size = src.shape[0] // pieces
        for p in range(pieces):
            at = pl.ds(p * size, size)
            moves.append(
                (
                    pltpu.make_async_copy(src.at[at], held.at[which, p], sem_in.at[which, p]),
                    pltpu.make_async_copy(held.at[which, p], dst.at[at], sem_out.at[which, p]),
                )
            )
    for load, _ in moves:
        load.start()
    for load, save in moves:
        load.wait()
        save.start()
    for _, save in moves:
        save.wait()


def store(new, mid):
    hbm = pl.BlockSpec(memory_space=pltpu.HBM)
    pieces = 2
    return pl.pallas_call(
        store_kernel,
        out_shape=(
            jax.ShapeDtypeStruct(new.shape, new.dtype),
            jax.ShapeDtypeStruct(mid.shape, mid.dtype),
        ),
        in_specs=[hbm, hbm],
        out_specs=(hbm, hbm),
        scratch_shapes=[
            pltpu.VMEM((2, pieces, new.shape[0] // pieces) + new.shape[1:], new.dtype),
            pltpu.SemaphoreType.DMA((2, pieces)),
            pltpu.SemaphoreType.DMA((2, pieces)),
        ],
        compiler_params=pltpu.CompilerParams(vmem_limit_bytes=VMEM_BYTES),
    )(new, mid)


def fits(mesh, pair_shape, hidden):
    n = mesh.shape["row"]
    rows = pair_shape[0] // (n * mesh.shape["grp"])
    tokens = pair_shape[1]
    aligned = rows % 8 == 0 and hidden % (8 * n) == 0 and tokens % 128 == 0
    aligned = aligned and hidden == pair_shape[2]
    small = hidden * rows * tokens * 40 <= 40 * 2**20
    return mesh.shape["kc"] == 1 and n > 1 and n & (n - 1) == 0 and n * rows == tokens and aligned and small


def solution(mesh):
    in_specs = (P(("grp", "row"), "kc", None), P(), P(), P(), P(), P(), P(), P())
    out_specs = (P(("grp", "row"), "kc", None), P(("grp", "row"), "kc", None))

    def run(*operands):
        if fits(mesh, operands[0].shape, operands[3].shape[1]):
            n = mesh.shape["row"]

            def body(*local):
                return store(*fused(n, *local))

        else:
            body = shards
        return jax.shard_map(
            body, mesh=mesh, in_specs=in_specs, out_specs=out_specs, check_vma=False
        )(*operands)

    return run
```

```python
import functools

import jax
import jax.numpy as jnp
from jax import lax
from jax.experimental import pallas as pl
from jax.experimental.pallas import tpu as pltpu
from jax.sharding import PartitionSpec as P


def layer_norm(values, gain, bias, axis_pos):
    center = jnp.mean(values, axis=axis_pos, keepdims=True)
    spread = jnp.mean((values - center) ** 2, axis=axis_pos, keepdims=True)
    return (values - center) * lax.rsqrt(spread + 1e-05) * gain + bias


def prepare(state, layer_index, w_in, w_gate, gain_in, bias_in):
    hidden = w_in.shape[2] // 4
    pair_float = state.astype(jnp.float32)
    normed = layer_norm(pair_float, gain_in[layer_index], bias_in[layer_index], 2).astype(
        jnp.bfloat16
    )
    projected = jnp.einsum(
        "ijc,ch->hij", normed, w_in[layer_index], preferred_element_type=jnp.float32
    )
    left = (jax.nn.sigmoid(projected[:hidden]) * projected[hidden : 2 * hidden]).astype(
        jnp.bfloat16
    )
    right = (jax.nn.sigmoid(projected[2 * hidden : 3 * hidden]) * projected[3 * hidden :]).astype(
        jnp.bfloat16
    )
    gate_values = jax.nn.sigmoid(
        jnp.einsum("ijc,cd->ijd", normed, w_gate[layer_index], preferred_element_type=jnp.float32)
    )
    return (pair_float, left, right, gate_values)


def finish(pair_float, gate_values, returned, layer_index, w_out, gain_mid, bias_mid):
    middle = layer_norm(
        returned.astype(jnp.float32),
        gain_mid[layer_index][:, None],
        bias_mid[layer_index][:, None],
        1,
    ).astype(jnp.bfloat16)
    branch = jnp.einsum(
        "jhi,hc->ijc", middle, w_out[layer_index], preferred_element_type=jnp.float32
    )
    return ((pair_float + gate_values * branch).astype(jnp.bfloat16), middle)


def shards(pair, w_in, w_gate, w_out, gain_in, bias_in, gain_mid, bias_mid):
    pair_float, left, right, gate_values = prepare(pair, 0, w_in, w_gate, gain_in, bias_in)
    left_c, right_c = (
        lax.all_to_all(left, "row", split_axis=0, concat_axis=1, tiled=True),
        lax.all_to_all(right, "row", split_axis=0, concat_axis=1, tiled=True),
    )
    right_rows = right_c
    summed = lax.psum_scatter(
        jnp.einsum("hjs,his->jhi", right_rows, left_c, preferred_element_type=jnp.float32).astype(
            jnp.bfloat16
        ),
        "kc",
        scatter_dimension=0,
        tiled=True,
    ).astype(jnp.float32)
    returned = lax.all_to_all(
        summed.astype(jnp.bfloat16), "row", split_axis=2, concat_axis=1, tiled=True
    )
    state, unused = finish(pair_float, gate_values, returned, 0, w_out, gain_mid, bias_mid)
    pair_float, left, right, gate_values = prepare(state, 1, w_in, w_gate, gain_in, bias_in)
    left_c, right_c = (
        lax.all_to_all(left, "row", split_axis=0, concat_axis=1, tiled=True),
        lax.all_to_all(right, "row", split_axis=0, concat_axis=1, tiled=True),
    )
    summed = jnp.einsum(
        "hpj,hpi->jhi",
        right_c,
        lax.all_gather(left_c, "kc", axis=2, tiled=True),
        preferred_element_type=jnp.float32,
    )
    returned = lax.all_to_all(
        summed.astype(jnp.bfloat16), "row", split_axis=2, concat_axis=1, tiled=True
    )
    final_state, middle = finish(pair_float, gate_values, returned, 1, w_out, gain_mid, bias_mid)
    return (final_state, middle.transpose(2, 0, 1))

MESH = pl.DeviceIdType.MESH
F32 = jnp.float32
BF16 = jnp.bfloat16
CHUNKS = 1
VMEM_BYTES = 64 * 2**20 - 2**16


def sigmoid(x):
    return 0.5 * jnp.tanh(0.5 * x) + 0.5


def norm_lanes(x, gain, bias):
    center = jnp.mean(x, axis=-1, keepdims=True)
    moved = x - center
    spread = jnp.mean(moved * moved, axis=-1, keepdims=True)
    return moved * lax.rsqrt(spread + 1e-05) * gain + bias


def fused_kernel(
    n,
    chunks,
    *refs,
):
    operands, refs = refs[:8], refs[8:]
    out_ref, mid_ref = refs[:2]
    loaded, refs = refs[2:10], refs[10:]
    (
        load_sem,
        w_t,
        state,
        normed,
        gate,
        lanes_l,
        lanes_r,
        send_a,
        recv_a,
        send_b,
        recv_b,
        sa_sem,
        ra_sem,
        sb_sem,
        rb_sem,
        out_buf,
        mid_buf,
        save_sem,
    ) = refs
    pending = []
    loads = [
        pltpu.make_async_copy(src, dst, load_sem.at[k])
        for k, (src, dst) in enumerate(zip(operands, loaded))
    ]
    for load in loads:
        load.start()
    (
        pair_ref,
        w_in_ref,
        w_gate_ref,
        w_out_ref,
        gain_in_ref,
        bias_in_ref,
        gain_mid_ref,
        bias_mid_ref,
    ) = loaded
    rows, tokens, channels = pair_ref.shape
    hidden = w_out_ref.shape[1]
    hb = hidden // n
    part = hb * rows
    per = hb // chunks
    piece = per * rows
    me = lax.axis_index("row")

    barrier = pltpu.get_barrier_semaphore()

    def greet(o, c):
        pl.semaphore_signal(
            barrier, inc=1, device_id={"row": lax.rem(me + o, n)}, device_id_type=MESH
        )
        return c

    lax.fori_loop(1, n, greet, 0)

    flips = []
    for bit in range(n.bit_length() - 1):
        size = 2**bit
        flips.append(size - 2 * size * lax.rem(lax.div(me, size), 2))

    def start_all(bufs, k, offsets):
        send, recv, ssem, rsem = bufs
        for o in offsets:
            other = me
            for bit, flip in enumerate(flips):
                if o // 2**bit % 2 == 1:
                    other = other + flip
            pltpu.make_async_remote_copy(
                src_ref=send.at[k, other],
                dst_ref=recv.at[k, me],
                send_sem=ssem.at[k],
                recv_sem=rsem.at[k],
                device_id={"row": other},
                device_id_type=MESH,
            ).start()

    def wait_all(bufs, k):
        send, recv, ssem, rsem = bufs
        blocks = recv.at[k, pl.ds(0, n - 1)]
        pltpu.make_async_copy(blocks, blocks, rsem.at[k]).wait()

    def drain(bufs, k):
        send, recv, ssem, rsem = bufs
        blocks = send.at[k, pl.ds(0, n - 1)]
        pltpu.make_async_copy(blocks, blocks, ssem.at[k]).wait()

    bufs_a = (send_a, recv_a, sa_sem, ra_sem)
    bufs_b = (send_b, recv_b, sb_sem, rb_sem)

    for k in (1, 4, 5, 0):
        loads[k].wait()
    w_t[0] = w_in_ref[0].T

    for u in range(2):
        source = pair_ref if u == 0 else state
        for i in range(rows):
            x = source[i].astype(F32)
            normed[i] = norm_lanes(
                x, gain_in_ref[u : u + 1, :], bias_in_ref[u : u + 1, :]
            ).astype(BF16)
        half, wide = n // 2, hidden // 2
        own_half = lax.div(me, half)
        for stage, side in enumerate((1 - own_half, own_half)):
            first = pl.multiple_of(side * wide, wide)
            weights = jnp.concatenate(
                [w_t[u, pl.ds(g * hidden + first, wide), :] for g in range(4)], axis=0
            )
            base = stage * wide * rows
            for i in range(rows):
                proj = lax.dot_general(
                    weights, normed[i], (((1,), (1,)), ((), ())), preferred_element_type=F32
                )
                at = pl.ds(base + i, wide, stride=rows)
                lanes_l[at, :] = sigmoid(proj[:wide]) * proj[wide : 2 * wide]
                lanes_r[at, :] = sigmoid(proj[2 * wide : 3 * wide]) * proj[3 * wide :]
            owners = pl.ds(side * half, half)
            part_of = slice(base, base + wide * rows)
            left = lanes_l[part_of, :].reshape(half, part, tokens)
            right = lanes_r[part_of, :].reshape(half, part, tokens)
            send_a[u, owners, :part, :] = left.astype(BF16)
            send_a[u, owners, part:, :] = right.astype(BF16)
            if u == 0 and stage == 0:
                pl.semaphore_wait(barrier, n - 1)
            start_all(bufs_a, u, range(n - 1, half - 1, -1) if stage == 0 else range(half - 1, 0, -1))
        for c in range(chunks):
            k = u * chunks + c
            recv_a[k, pl.ds(me, 1)] = send_a[k, pl.ds(me, 1)]
        if u == 0:
            w_t[1] = w_in_ref[1].T
            for k in (2, 3, 6, 7):
                loads[k].wait()
        for i in range(rows):
            gate[i] = sigmoid(jnp.dot(normed[i], w_gate_ref[u], preferred_element_type=F32))
        dims = (((1,), (1,)), ((), ())) if u == 0 else (((0,), (0,)), ((), ()))
        for c in range(chunks):
            k = u * chunks + c
            wait_all(bufs_a, k)
            for p in range(per // 2):
                pair_of = slice(2 * p * rows, 2 * (p + 1) * rows)
                lblk = recv_a[k, :, pair_of, :].astype(F32)
                rblk = recv_a[k, :, piece + 2 * p * rows : piece + 2 * (p + 1) * rows, :].astype(F32)
                tri = []
                for q in range(2):
                    cut = slice(q * rows, (q + 1) * rows)
                    lh = lblk[:, cut, :].reshape(n * rows, tokens).astype(BF16)
                    rh = rblk[:, cut, :].reshape(n * rows, tokens).astype(BF16)
                    one = lax.dot_general(lh, rh, dims, preferred_element_type=F32)
                    tri.append(one.reshape(n, rows, tokens))
                send_b[k, :, pair_of, :] = jnp.concatenate(tri, axis=1).astype(BF16)
            start_all(bufs_b, k, range(n - 1, 0, -1))
            recv_b[k, pl.ds(me, 1)] = send_b[k, pl.ds(me, 1)]
        for c in range(chunks):
            k = u * chunks + c
            drain(bufs_a, k)
            if u == 1:
                drain(bufs_b, c)
            wait_all(bufs_b, k)
            for d in range(n):
                at = d * part + c * piece
                lanes_l[at : at + piece, :] = recv_b[k, d].astype(F32)
        for i in range(rows):
            tri = lanes_l[pl.ds(i, hidden, stride=rows), :].T
            mid = norm_lanes(
                tri, gain_mid_ref[u : u + 1, :], bias_mid_ref[u : u + 1, :]
            ).astype(BF16)
            branch = jnp.dot(mid, w_out_ref[u], preferred_element_type=F32)
            new = (source[i].astype(F32) + gate[i] * branch).astype(BF16)
            if u == 0:
                state[i] = new
            else:
                out_buf[i] = new
                mid_buf[i] = mid
                saves = [
                    pltpu.make_async_copy(out_buf.at[i], out_ref.at[i], save_sem.at[0, i]),
                    pltpu.make_async_copy(mid_buf.at[i], mid_ref.at[i], save_sem.at[1, i]),
                ]
                for save in saves:
                    save.start()
                pending.extend(saves)
    for save in pending:
        save.wait()
    for k in range(chunks, 2 * chunks):
        drain(bufs_b, k)


def fused(n, *operands):
    pair, hidden = operands[0], operands[3].shape[1]
    rows, tokens, channels = pair.shape
    chunks = CHUNKS if hidden // n % (2 * CHUNKS) == 0 else 1
    piece = hidden // n * rows // chunks
    vmem = pl.BlockSpec(memory_space=pltpu.VMEM)
    return pl.pallas_call(
        functools.partial(fused_kernel, n, chunks),
        out_shape=(
            jax.ShapeDtypeStruct(pair.shape, BF16),
            jax.ShapeDtypeStruct((rows, tokens, hidden), BF16),
        ),
        in_specs=[pl.BlockSpec(memory_space=pltpu.HBM)] * len(operands),
        out_specs=(pl.BlockSpec(memory_space=pltpu.HBM),) * 2,
        scratch_shapes=[pltpu.VMEM(operand.shape, operand.dtype) for operand in operands]
        + [
            pltpu.SemaphoreType.DMA((len(operands),)),
            pltpu.VMEM((2, 4 * hidden, channels), BF16),
            pltpu.VMEM(pair.shape, BF16),
            pltpu.VMEM(pair.shape, BF16),
            pltpu.VMEM(pair.shape, F32),
            pltpu.VMEM((hidden * rows, tokens), F32),
            pltpu.VMEM((hidden * rows, tokens), F32),
            pltpu.VMEM((2 * chunks, n, 2 * piece, tokens), BF16),
            pltpu.VMEM((2 * chunks, n, 2 * piece, tokens), BF16),
            pltpu.VMEM((2 * chunks, n, piece, tokens), BF16),
            pltpu.VMEM((2 * chunks, n, piece, tokens), BF16),
        ]
        + [pltpu.SemaphoreType.DMA((2 * chunks,))] * 4
        + [
            pltpu.VMEM(pair.shape, BF16),
            pltpu.VMEM((rows, tokens, hidden), BF16),
            pltpu.SemaphoreType.DMA((2, rows)),
        ],
        compiler_params=pltpu.CompilerParams(
            collective_id=0, has_side_effects=True, vmem_limit_bytes=VMEM_BYTES
        ),
    )(*operands)


def store_kernel(new_ref, mid_ref, out_ref, out_mid_ref, held, sem_in, sem_out):
    pieces = held.shape[1]
    moves = []
    for which, (src, dst) in enumerate(((new_ref, out_ref), (mid_ref, out_mid_ref))):
        size = src.shape[0] // pieces
        for p in range(pieces):
            at = pl.ds(p * size, size)
            moves.append(
                (
                    pltpu.make_async_copy(src.at[at], held.at[which, p], sem_in.at[which, p]),
                    pltpu.make_async_copy(held.at[which, p], dst.at[at], sem_out.at[which, p]),
                )
            )
    for load, _ in moves:
        load.start()
    for load, save in moves:
        load.wait()
        save.start()
    for _, save in moves:
        save.wait()


def store(new, mid):
    hbm = pl.BlockSpec(memory_space=pltpu.HBM)
    pieces = 2
    return pl.pallas_call(
        store_kernel,
        out_shape=(
            jax.ShapeDtypeStruct(new.shape, new.dtype),
            jax.ShapeDtypeStruct(mid.shape, mid.dtype),
        ),
        in_specs=[hbm, hbm],
        out_specs=(hbm, hbm),
        scratch_shapes=[
            pltpu.VMEM((2, pieces, new.shape[0] // pieces) + new.shape[1:], new.dtype),
            pltpu.SemaphoreType.DMA((2, pieces)),
            pltpu.SemaphoreType.DMA((2, pieces)),
        ],
        compiler_params=pltpu.CompilerParams(vmem_limit_bytes=VMEM_BYTES),
    )(new, mid)


def fits(mesh, pair_shape, hidden):
    n = mesh.shape["row"]
    rows = pair_shape[0] // (n * mesh.shape["grp"])
    tokens = pair_shape[1]
    aligned = rows % 8 == 0 and hidden % (8 * n) == 0 and tokens % 128 == 0
    aligned = aligned and hidden == pair_shape[2]
    small = hidden * rows * tokens * 40 <= 40 * 2**20
    return mesh.shape["kc"] == 1 and n > 1 and n & (n - 1) == 0 and n * rows == tokens and aligned and small


def solution(mesh):
    in_specs = (P(("grp", "row"), "kc", None), P(), P(), P(), P(), P(), P(), P())
    out_specs = (P(("grp", "row"), "kc", None), P(("grp", "row"), "kc", None))

    def run(*operands):
        if fits(mesh, operands[0].shape, operands[3].shape[1]):
            n = mesh.shape["row"]

            def body(*local):
                return store(*fused(n, *local))

        else:
            body = shards
        return jax.shard_map(
            body, mesh=mesh, in_specs=in_specs, out_specs=out_specs, check_vma=False
        )(*operands)

    return run
```
